256 devices in a mesh: inner: 8 (over y_hi, x), outer: 16 (over y_lo, z), head: 2 (over core).
Axes of the slice: x: 4, y: 4 (y_hi: 2, y_lo: 2; y = y_hi * 2 + y_lo), z: 8, core: 2. Of those that a mesh axis runs over, the one named last changes fastest.
Arguments:
- queries: bfloat16 [16384, 4096], P(('inner', 'outer'), 'head'), may hold values from -6 to 6
- out_grad: bfloat16 [16384, 4096], P(('inner', 'outer'), 'head'), may hold values from -6 to 6
- outputs: bfloat16 [16384, 4096], P(('inner', 'outer'), 'head'), may hold values from -4 to 4
- log_norm: float32 [32, 16384], P('head', ('inner', 'outer')), may hold values from 4 to 6
- kv_held: bfloat16 [16384, 2, 512], P(('inner', 'outer'), None, 'head'), may hold values from -6 to 6
- span_order: int32 [256], replicated, may hold values from 0 to 255, each once
- dq_acc: float32 [16384, 4096], P(('inner', 'outer'), 'head'), may hold values from -6 to 6
- dkv_acc: float32 [16384, 2, 512], P(('inner', 'outer'), None, 'head'), may hold values from -6 to 6
- kv_weight: bfloat16 [8192, 2, 512], P(('inner', 'outer'), None, 'head'), may hold values from -0.1875 to 0.1875
Outputs:
- dq: float32 [16384, 4096], P(('inner', 'outer'), 'head')
- dkv: float32 [16384, 2, 512], P(('inner', 'outer'), None, 'head')
- dx: bfloat16 [16384, 8192], P(('inner', 'outer'), 'head')
The draws below stay inside these ranges and needn't reach their ends.
Inputs may be any that keep to these rules, and one draw needn't show every extreme that they name: `span_order`: every block number appears exactly once.
All inputs are finite; a program needn't handle non-finite values.
Results may differ from the reference program's by a relative error of at most 0.0056.
Values may be sent and summed in bfloat16 or wider, within the bound.
No kernel may reach another device: no remote copies, remote signals or barrier semaphores. Data moves between devices by JAX's collectives and lax.ppermute only.
A program may use at most 128 MiB of HBM per device.

```python
import math
import jax
import jax.numpy as jnp
from jax import lax

HD = 128
QH = 32
KVH = 4
D = 8192
SPAN = 64
SPANS = 256
TOKENS = 16384
N_INNER = 8
N_OUTER = 16


def level_of(own_key, extent, pieces, least, high):
    def one(position, shards_of):
        draws = jax.random.uniform(jax.random.fold_in(jax.random.fold_in(own_key, 6), position), (shards_of,), jnp.float32, least / len(pieces), high / len(pieces))
        return jnp.repeat(jnp.exp(draws), extent[position] // shards_of).reshape((-1,) + (1,) * (len(extent) - position - 1))

    level = one(*pieces[0])
    for cut in pieces[1:]:
        level = level * one(*cut)
    return level


def centred(rng, dims, scale, bound, split=(), kind=jnp.bfloat16):
    drawn = jax.random.normal(rng, dims, jnp.float32) * scale
    if len(split) > 0:
        drawn = level_of(rng, dims, split, -0.22, 0.18) * drawn
    return jnp.clip(drawn, min=-bound, max=bound).astype(kind)


def setup_inputs(seed: int = 0) -> dict:
    splits = jax.random.split(jax.random.key(seed), 10)
    queries = centred(splits[0], (TOKENS, QH * HD), 1.0, 6.0, ((0, 128), (1, 2)))
    out_grad = centred(splits[1], (TOKENS, QH * HD), 1.0, 6.0, ((0, 128), (1, 2)))
    outputs = centred(splits[2], (TOKENS, QH * HD), 0.3, 4.0, ((0, 128), (1, 2)))
    log_norm = jnp.clip(4.0 + 2.0 * jax.random.uniform(splits[3], (QH, TOKENS), jnp.float32) ** level_of(splits[3], (QH, TOKENS), ((0, 2), (1, 128)), -0.2, 0.2), 4.0, 6.0)
    kv_held = centred(splits[4], (TOKENS, 2, KVH * HD), 1.0, 6.0, ((0, 128), (2, 2)))
    span_order = jax.random.permutation(splits[5], SPANS).astype(jnp.int32)
    dq_acc = centred(splits[6], (TOKENS, QH * HD), 0.5, 6.0, ((0, 128), (1, 2)), jnp.float32)
    dkv_acc = centred(splits[7], (TOKENS, 2, KVH * HD), 1.0, 6.0, ((0, 128), (2, 2)), jnp.float32)
    kv_weight = centred(splits[8], (D, 2, KVH * HD), (2 * KVH * HD) ** -0.5, 0.1875, ((0, 128), (2, 2)))
    return {"queries": queries, "out_grad": out_grad, "outputs": outputs, "log_norm": log_norm, "kv_held": kv_held, "span_order": span_order, "dq_acc": dq_acc, "dkv_acc": dkv_acc, "kv_weight": kv_weight}


def reference(queries, out_grad, outputs, log_norm, kv_held, span_order, dq_acc, dkv_acc, kv_weight):
    rows = 2 * SPAN
    group_size = QH // KVH
    scale = 1.0 / math.sqrt(HD)
    positions = (span_order[:, None] * SPAN + jnp.arange(SPAN, dtype=jnp.int32)[None, :]).reshape(-1).astype(jnp.int32)
    key_positions = jnp.roll(positions.reshape(N_INNER, N_OUTER, rows), -1, axis=1).reshape(-1)

    def grouped(x):
        rest = x.shape[1:]
        y = x.reshape((N_INNER, N_OUTER, rows) + rest)
        y = jnp.swapaxes(y, 0, 1)
        return y.reshape((N_OUTER, N_INNER * rows) + rest)

    def ungroup(x):
        rest = x.shape[2:]
        y = x.reshape((N_OUTER, N_INNER, rows) + rest)
        y = jnp.swapaxes(y, 0, 1)
        return y.reshape((TOKENS,) + rest)

    def one_group(items):
        qblk, doblk, oblk, lblk, kvblk, qpos, kpos = items
        width = qblk.shape[0]
        allowed = kpos[None, :] <= qpos[:, None]
        q4 = qblk.astype(jnp.float32).reshape(width, KVH, group_size, HD).transpose(1, 0, 2, 3)
        do4 = doblk.astype(jnp.float32).reshape(width, KVH, group_size, HD).transpose(1, 0, 2, 3)
        o4 = oblk.astype(jnp.float32).reshape(width, KVH, group_size, HD).transpose(1, 0, 2, 3)
        lse3 = lblk.reshape(width, KVH, group_size).transpose(1, 2, 0)
        keys = kvblk[:, 0].astype(jnp.float32).reshape(width, KVH, HD).transpose(1, 0, 2)
        values = kvblk[:, 1].astype(jnp.float32).reshape(width, KVH, HD).transpose(1, 0, 2)

        def one_head(hitems):
            qh, doh, oh, lseh, kh, vh = hitems
            scores = jnp.einsum('tgc,uc->gtu', qh, kh) * scale
            prob = jnp.where(allowed[None], jnp.exp(scores - lseh[:, :, None]), 0.0)
            probb = prob.astype(jnp.bfloat16).astype(jnp.float32)
            delta = jnp.einsum('tgc,tgc->gt', doh, oh)
            dprob = jnp.einsum('tgc,uc->gtu', doh, vh)
            dscore = (prob * (dprob - delta[:, :, None])).astype(jnp.bfloat16).astype(jnp.float32)
            dq_h = jnp.einsum('gtu,uc->tgc', dscore, kh) * scale
            dk_h = jnp.einsum('gtu,tgc->uc', dscore, qh) * scale
            dv_h = jnp.einsum('gtu,tgc->uc', probb, doh)
            return (dq_h, dk_h, dv_h)
        dq_g, dk_g, dv_g = lax.map(one_head, (q4, do4, o4, lse3, keys, values))
        dq_g = dq_g.transpose(1, 0, 2, 3).reshape(width, QH * HD)
        dk_g = dk_g.transpose(1, 0, 2).reshape(width, KVH * HD)
        dv_g = dv_g.transpose(1, 0, 2).reshape(width, KVH * HD)
        return (dq_g, jnp.stack([dk_g, dv_g], axis=1))
    items = (grouped(queries), grouped(out_grad), grouped(outputs), grouped(log_norm.T), grouped(kv_held), grouped(positions), grouped(key_positions))
    dq_terms, dkv_terms = lax.map(one_group, items)
    dq = dq_acc + ungroup(dq_terms)
    held_terms = ungroup(dkv_terms).reshape(N_INNER, N_OUTER, rows, 2, KVH * HD)
    owned_terms = jnp.roll(held_terms, 1, axis=1).reshape(TOKENS, 2, KVH * HD)
    dkv = dkv_acc + owned_terms
    dkvb = dkv.astype(jnp.bfloat16).reshape(TOKENS, 2 * KVH * HD)
    weight_flat = kv_weight.reshape(D, 2 * KVH * HD)
    dx = jnp.dot(dkvb, weight_flat.T, preferred_element_type=jnp.float32).astype(jnp.bfloat16)
    return (dq, dkv, dx)
```

```python
import math

import jax
import jax.numpy as jnp
from jax import lax
from jax.experimental import pallas as pl
from jax.experimental.pallas import tpu as pltpu
from jax.sharding import Mesh, PartitionSpec as P

HD = 128
SPAN = 64
ROWS = 128
AXES = ("yh", "x", "yl", "z", "core")
SIZES = (2, 4, 2, 8, 2)
LOG2E = math.log2(math.e)
SCALE = 1.0 / math.sqrt(HD)
F32 = jnp.float32
BF16 = jnp.bfloat16
MIB = 1 << 20


def permute(value, move):
    pairs = []
    for a in range(2):
        for x in range(4):
            for b in range(2):
                for z in range(8):
                    for h in range(2):
                        flat = lambda c: (((c[0] * 4 + c[1]) * 2 + c[2]) * 8 + c[3]) * 2 + c[4]
                        pairs.append((flat((a, x, b, z, h)), flat(move(a, x, b, z, h))))
    return lax.ppermute(value, AXES, pairs)


def along_x(steps):
    return lambda a, x, b, z, h: (a, (x + steps) % 4, b, z, h)


def ring4(steps, core_zero_on_x):
    def move(a, x, b, z, h):
        if (h == 0) == core_zero_on_x:
            return (a, (x + steps) % 4, b, z, h)
        y = (a * 2 + b + steps) % 4
        return (y // 2, x, y % 2, z, h)

    return move


def next_outer(flip):
    def move(a, x, b, z, h):
        g = (b * 8 + z + 1) % 16
        return (a ^ flip, x, g // 8, g % 8, h)

    return move


def delta_body(do_ref, o_ref, lse_ref, delta_ref, lse2_ref):
    ones = jnp.ones((8, HD), F32)
    for h in range(16):
        cols = slice(h * HD, (h + 1) * HD)
        prod = do_ref[:, cols].astype(F32) * o_ref[:, cols].astype(F32)
        row = lax.dot_general(
            ones, prod, (((1,), (1,)), ((), ())),
            precision=lax.Precision.HIGHEST, preferred_element_type=F32,
        )
        delta_ref[h : h + 1, :] = row[0:1]
    lse2_ref[...] = lse_ref[...] * LOG2E


def attend_body(shift, spans, q_ref, do_ref, lse_ref, delta_ref, kv_ref, dqin_ref, terms_ref, dq_ref, dk_s, dv_s):
    head = pl.program_id(0)
    part = pl.program_id(1)
    yh = lax.axis_index("yh")
    x = lax.axis_index("x")
    outer = lax.axis_index("yl") * 8 + lax.axis_index("z")
    mine = (yh * 4 + x) * 16 + outer
    key_outer = lax.rem(outer + 1, 16)
    key_x = lax.rem(x + 4 - shift, 4)
    first = (yh * 4 + key_x) * 16 + key_outer
    second = ((1 - yh) * 4 + key_x) * 16 + key_outer
    lane = lax.broadcasted_iota(jnp.int32, (1, ROWS), 1)
    q_pos = jnp.where(lane < SPAN, spans[2 * mine] * SPAN + lane, spans[2 * mine + 1] * SPAN + lane - SPAN)
    row = lax.broadcasted_iota(jnp.int32, (2 * ROWS, 1), 0)
    k_span = jnp.where(
        row < 2 * SPAN,
        jnp.where(row < SPAN, spans[2 * first], spans[2 * first + 1]),
        jnp.where(row < 3 * SPAN, spans[2 * second], spans[2 * second + 1]),
    )
    k_pos = k_span * SPAN + lax.rem(row, SPAN)
    allowed = k_pos <= q_pos
    allowed = jnp.concatenate([allowed, allowed], axis=1)
    at = pl.ds(pl.multiple_of(head * HD, HD), HD)
    at_v = pl.ds(pl.multiple_of(head * HD + 2 * HD, HD), HD)
    keys = jnp.concatenate([kv_ref[0, :, at], kv_ref[1, :, at]], axis=0)
    values = jnp.concatenate([kv_ref[0, :, at_v], kv_ref[1, :, at_v]], axis=0)
    nt = (((1,), (1,)), ((), ()))
    dk = None
    for pair in range(2):
        c0 = slice(pair * 256, pair * 256 + 128)
        c1 = slice(pair * 256 + 128, pair * 256 + 256)
        h0 = head * 8 + part * 4 + pair * 2
        q2 = jnp.concatenate([q_ref[:, c0], q_ref[:, c1]], axis=0)
        do2 = jnp.concatenate([do_ref[:, c0], do_ref[:, c1]], axis=0)
        lse = jnp.concatenate([lse_ref[pl.ds(h0, 1), :], lse_ref[pl.ds(h0 + 1, 1), :]], axis=1)
        delta = jnp.concatenate([delta_ref[pl.ds(h0, 1), :], delta_ref[pl.ds(h0 + 1, 1), :]], axis=1)
        s = lax.dot_general(keys, q2, nt, preferred_element_type=F32)
        p = jnp.where(allowed, jnp.exp2(s * (SCALE * LOG2E) - lse), 0.0)
        dp = lax.dot_general(values, do2, nt, preferred_element_type=F32)
        ds = (p * (dp - delta)).astype(BF16)
        pb = p.astype(BF16)
        dv_t = jnp.dot(pb, do2, preferred_element_type=F32)
        dk_t = jnp.dot(ds, q2, preferred_element_type=F32)
        dk = dk_t if dk is None else dk + dk_t
        dv = dv_t if pair == 0 else dv + dv_t
        dq = lax.dot_general(ds, keys, (((0,), (0,)), ((), ())), preferred_element_type=F32)
        dq_ref[:, c0] = dqin_ref[:, c0] + dq[:ROWS] * SCALE
        dq_ref[:, c1] = dqin_ref[:, c1] + dq[ROWS:] * SCALE

    @pl.when(part == 0)
    def _():
        dk_s[...] = dk
        dv_s[...] = dv

    @pl.when(part == 1)
    def _():
        k = ((dk_s[...] + dk) * SCALE).astype(BF16)
        v = (dv_s[...] + dv).astype(BF16)
        terms_ref[0, :, at] = k[:ROWS]
        terms_ref[1, :, at] = k[ROWS:]
        terms_ref[0, :, at_v] = v[:ROWS]
        terms_ref[1, :, at_v] = v[ROWS:]


def attend(shift, spans, q, do, lse2, delta, kvp, dq_in, alias):
    half = lambda i, j, s: (0, i * 2 + j)
    whole2 = lambda i, j, s: (0, 0)
    return pl.pallas_call(
        lambda *refs: attend_body(shift, *refs),
        grid_spec=pltpu.PrefetchScalarGridSpec(
            num_scalar_prefetch=1,
            grid=(2, 2),
            in_specs=[
                pl.BlockSpec((ROWS, 512), half),
                pl.BlockSpec((ROWS, 512), half),
                pl.BlockSpec((16, ROWS), whole2),
                pl.BlockSpec((16, ROWS), whole2),
                pl.BlockSpec((2, ROWS, 512), lambda i, j, s: (0, 0, 0)),
                pl.BlockSpec((ROWS, 512), half),
            ],
            out_specs=[
                pl.BlockSpec((2, ROWS, 512), lambda i, j, s: (0, 0, 0)),
                pl.BlockSpec((ROWS, 512), half),
            ],
            scratch_shapes=[pltpu.VMEM((256, HD), F32), pltpu.VMEM((256, HD), F32)],
        ),
        out_shape=[
            jax.ShapeDtypeStruct((2, ROWS, 512), BF16),
            jax.ShapeDtypeStruct((ROWS, 2048), F32),
        ],
        input_output_aliases={6: 1} if alias else {},
        compiler_params=pltpu.CompilerParams(vmem_limit_bytes=24 * MIB),
        cost_estimate=pl.CostEstimate(flops=700_000_000, bytes_accessed=4_000_000, transcendentals=524288),
        name="attend",
    )(spans, q, do, lse2, delta, kvp, dq_in)


def reduce_body(t0, t1, t2, t3, r0, r1):
    total = t0[...].astype(F32) + t1[...].astype(F32) + t2[...].astype(F32) + t3[...].astype(F32)
    total = total.astype(BF16)
    r0[...] = total[0]
    r1[...] = total[1]


def final_body(acc, r0, r1, dkv, dkvb):
    total = acc[...] + (r0[...].astype(F32) + r1[...].astype(F32))
    dkv[...] = total
    dkvb[...] = total.astype(BF16)


def dx_body(own_ref, other_ref, *refs):
    a_refs, b_refs = refs[:8], refs[8:12]
    out_ref, wa, wb, dk, sems = refs[12:]
    yh = lax.axis_index("yh")
    x = lax.axis_index("x")
    yl = lax.axis_index("yl")
    z = lax.axis_index("z")
    core = lax.axis_index("core")
    y = yh * 2 + yl
    copies = [pltpu.make_async_copy(r, wa.at[k], sems.at[k]) for k, r in enumerate(a_refs)]
    copies += [pltpu.make_async_copy(r, wb.at[k], sems.at[8 + k]) for k, r in enumerate(b_refs)]
    for c in copies:
        c.start()
    dk[core] = own_ref[...]
    dk[1 - core] = other_ref[...]
    for c in copies:
        c.wait()
    nt = (((1,), (1,)), ((), ()))
    p_at = jnp.where(core == 0, x, y)
    q_at = jnp.where(core == 0, y, x)

    @pl.loop(0, 16)
    def _(tile):
        tx = tile // 4
        tb = lax.rem(tile // 2, 2)
        tz = lax.rem(tile, 2) * 4
        total = None
        for a in range(2):
            ty = a * 2 + tb
            p_to = jnp.where(core == 0, tx, ty)
            q_to = jnp.where(core == 0, ty, tx)
            s = lax.rem(p_at - p_to + 4, 4)
            t = lax.rem(q_at - q_to + 4, 4)
            wa_rows = []
            wb_rows = []
            for m in range(4):
                zz = tz + m
                k = jnp.where(core == 0, lax.rem(z - zz + 8, 8), lax.rem(zz - z + 8, 8))
                wa_rows.append(wa[k, t * 4 + s])
                e = lax.bitwise_xor(z, zz)
                wb_rows.append(wb[t, s * 8 + e])
            w_a = jnp.concatenate(wa_rows, axis=0)
            w_b = jnp.concatenate(wb_rows, axis=0)
            got = lax.dot_general(dk[a, :, 0:256], w_a, nt, preferred_element_type=F32)
            got = got + lax.dot_general(dk[a, :, 256:512], w_b, nt, preferred_element_type=F32)
            total = got if total is None else total + got
        out_ref[:, pl.ds(pl.multiple_of(tile * 256, 256), 256)] = total.astype(BF16)


def shards(queries, out_grad, outputs, log_norm, kv_held, span_order, dq_acc, dkv_acc, kv_weight):
    vmem = pl.BlockSpec(memory_space=pltpu.VMEM)

    w0 = permute(kv_weight.reshape(64, 512), lambda a, x, b, z, h: (h, x, b, z, a))
    kv0 = kv_held.reshape(ROWS, 512)
    kvy = permute(kv0, lambda a, x, b, z, h: (1 - a, x, b, z, h))
    delta, lse2 = pl.pallas_call(
        delta_body,
        in_specs=[vmem] * 3,
        out_specs=[vmem] * 2,
        out_shape=[jax.ShapeDtypeStruct((16, ROWS), F32)] * 2,
        cost_estimate=pl.CostEstimate(flops=10_000_000, bytes_accessed=1_000_000, transcendentals=0),
        name="row_sums",
    )(out_grad, outputs, log_norm)
    pair = jnp.stack([kv0, kvy])
    pairs = {s: permute(pair, along_x(s)) for s in (1, 3, 2)}

    wa = w0[:, :256]
    wb = w0[:, 256:]
    a1 = jnp.stack([wa] + [permute(wa, ring4(s, True)) for s in (1, 2, 3)])
    for bit in (1, 2, 4):
        cur = wb[None] if bit == 1 else cur
        got = permute(cur, lambda a, x, b, z, h: (a, x, b, z ^ bit, h))
        cur = jnp.concatenate([cur, got], axis=0)
    a2 = jnp.concatenate([a1] + [permute(a1, ring4(s, False)) for s in (1, 2, 3)], axis=0)
    b2 = jnp.concatenate([cur] + [permute(cur, ring4(s, True)) for s in (1, 2, 3)], axis=0)
    b_parts = [b2] + [permute(b2, ring4(s, False)) for s in (1, 2, 3)]
    a_parts = [a2]
    for _ in range(7):
        a_parts.append(permute(a_parts[-1], lambda a, x, b, z, h: (a, x, b, (z + 1 - 2 * h) % 8, h)))

    t0, dq = attend(0, span_order, queries, out_grad, lse2, delta, pair, dq_acc, False)
    back = [t0]
    for s in (1, 3, 2):
        term, dq = attend(s, span_order, queries, out_grad, lse2, delta, pairs[s], dq, True)
        back.append(permute(term, along_x(-s)))
    r0, r1 = pl.pallas_call(
        reduce_body,
        in_specs=[vmem] * 4,
        out_specs=[vmem] * 2,
        out_shape=[jax.ShapeDtypeStruct((ROWS, 512), BF16)] * 2,
        cost_estimate=pl.CostEstimate(flops=1_000_000, bytes_accessed=1_300_000, transcendentals=0),
        name="reduce_terms",
    )(*back)
    r0 = permute(r0, next_outer(0))
    r1 = permute(r1, next_outer(1))
    dkv, dkvb = pl.pallas_call(
        final_body,
        in_specs=[vmem] * 3,
        out_specs=[vmem] * 2,
        out_shape=[jax.ShapeDtypeStruct((ROWS, 512), F32), jax.ShapeDtypeStruct((ROWS, 512), BF16)],
        cost_estimate=pl.CostEstimate(flops=1_000_000, bytes_accessed=1_000_000, transcendentals=0),
        name="add_terms",
    )(dkv_acc.reshape(ROWS, 512), r0, r1)
    other = permute(dkvb, lambda a, x, b, z, h: (a, x, b, z, 1 - h))
    dx = pl.pallas_call(
        dx_body,
        in_specs=[vmem] * 2 + [pl.BlockSpec(memory_space=pl.ANY)] * 12,
        out_specs=vmem,
        out_shape=jax.ShapeDtypeStruct((ROWS, 4096), BF16),
        scratch_shapes=[
            pltpu.VMEM((8, 16, 64, 256), BF16),
            pltpu.VMEM((4, 32, 64, 256), BF16),
            pltpu.VMEM((2, ROWS, 512), BF16),
            pltpu.SemaphoreType.DMA((12,)),
        ],
        compiler_params=pltpu.CompilerParams(vmem_limit_bytes=32 * MIB),
        cost_estimate=pl.CostEstimate(flops=1_100_000_000, bytes_accessed=9_000_000, transcendentals=0),
        name="input_grad",
    )(dkvb, other, *a_parts, *b_parts)
    return (dq, dkv.reshape(ROWS, 2, 256), dx)


def solution(mesh):
    fine = Mesh(mesh.devices.reshape(SIZES), AXES)
    tokens = ("yh", "x", "yl", "z")
    return jax.shard_map(
        shards,
        mesh=fine,
        in_specs=(
            P(tokens, "core"),
            P(tokens, "core"),
            P(tokens, "core"),
            P("core", tokens),
            P(tokens, None, "core"),
            P(),
            P(tokens, "core"),
            P(tokens, None, "core"),
            P(tokens, None, "core"),
        ),
        out_specs=(P(tokens, "core"), P(tokens, None, "core"), P(tokens, "core")),
        check_vma=False,
    )
```

```python
import math

import jax
import jax.numpy as jnp
from jax import lax
from jax.experimental import pallas as pl
from jax.experimental.pallas import tpu as pltpu
from jax.sharding import Mesh, PartitionSpec as P

HD = 128
SPAN = 64
ROWS = 128
AXES = ("yh", "x", "yl", "z", "core")
SIZES = (2, 4, 2, 8, 2)
LOG2E = math.log2(math.e)
SCALE = 1.0 / math.sqrt(HD)
F32 = jnp.float32
BF16 = jnp.bfloat16
MIB = 1 << 20
SMALL = pl.CostEstimate(flops=1000, bytes_accessed=1000, transcendentals=0)


def permute(value, move):
    pairs = []
    for a in range(2):
        for x in range(4):
            for b in range(2):
                for z in range(8):
                    for h in range(2):
                        flat = lambda c: (((c[0] * 4 + c[1]) * 2 + c[2]) * 8 + c[3]) * 2 + c[4]
                        pairs.append((flat((a, x, b, z, h)), flat(move(a, x, b, z, h))))
    return lax.ppermute(value, AXES, pairs)


def along_x(steps):
    return lambda a, x, b, z, h: (a, (x + steps) % 4, b, z, h)


def next_outer(flip):
    def move(a, x, b, z, h):
        g = (b * 8 + z + 1) % 16
        return (a ^ flip, x, g // 8, g % 8, h)

    return move


def delta_body(do_ref, o_ref, lse_ref, delta_ref, lse2_ref):
    ones = jnp.ones((8, HD), F32)
    for h in range(16):
        cols = slice(h * HD, (h + 1) * HD)
        prod = do_ref[:, cols].astype(F32) * o_ref[:, cols].astype(F32)
        row = lax.dot_general(
            ones, prod, (((1,), (1,)), ((), ())),
            precision=lax.Precision.HIGHEST, preferred_element_type=F32,
        )
        delta_ref[h : h + 1, :] = row[0:1]
    lse2_ref[...] = lse_ref[...] * LOG2E


def attend_body(shift, spans, q_ref, do_ref, lse_ref, delta_ref, kv_ref, dqin_ref, terms_ref, dq_ref):
    yh = lax.axis_index("yh")
    x = lax.axis_index("x")
    outer = lax.axis_index("yl") * 8 + lax.axis_index("z")
    mine = (yh * 4 + x) * 16 + outer
    key_outer = lax.rem(outer + 1, 16)
    key_x = lax.rem(x + 4 - shift, 4)
    first = (yh * 4 + key_x) * 16 + key_outer
    second = ((1 - yh) * 4 + key_x) * 16 + key_outer
    lane = lax.broadcasted_iota(jnp.int32, (1, ROWS), 1)
    q_pos = jnp.where(lane < SPAN, spans[2 * mine] * SPAN + lane, spans[2 * mine + 1] * SPAN + lane - SPAN)
    row = lax.broadcasted_iota(jnp.int32, (2 * ROWS, 1), 0)
    k_span = jnp.where(
        row < 2 * SPAN,
        jnp.where(row < SPAN, spans[2 * first], spans[2 * first + 1]),
        jnp.where(row < 3 * SPAN, spans[2 * second], spans[2 * second + 1]),
    )
    k_pos = k_span * SPAN + lax.rem(row, SPAN)
    allowed = k_pos <= q_pos
    allowed = jnp.concatenate([allowed, allowed], axis=1)
    nt = (((1,), (1,)), ((), ()))
    for head in range(2):
        at = slice(head * HD, (head + 1) * HD)
        at_v = slice(head * HD + 2 * HD, head * HD + 3 * HD)
        keys = jnp.concatenate([kv_ref[0, :, at], kv_ref[1, :, at]], axis=0)
        values = jnp.concatenate([kv_ref[0, :, at_v], kv_ref[1, :, at_v]], axis=0)
        dk = dv = None
        for pair in range(4):
            h0 = head * 8 + pair * 2
            c0 = slice(h0 * HD, (h0 + 1) * HD)
            c1 = slice((h0 + 1) * HD, (h0 + 2) * HD)
            q2 = jnp.concatenate([q_ref[:, c0], q_ref[:, c1]], axis=0)
            do2 = jnp.concatenate([do_ref[:, c0], do_ref[:, c1]], axis=0)
            lse = jnp.concatenate([lse_ref[h0 : h0 + 1, :], lse_ref[h0 + 1 : h0 + 2, :]], axis=1)
            delta = jnp.concatenate([delta_ref[h0 : h0 + 1, :], delta_ref[h0 + 1 : h0 + 2, :]], axis=1)
            s = lax.dot_general(keys, q2, nt, preferred_element_type=F32)
            dp = lax.dot_general(values, do2, nt, preferred_element_type=F32)
            p = jnp.where(allowed, jnp.exp2(s * (SCALE * LOG2E) - lse), 0.0)
            pb = p.astype(BF16)
            ds = (p * (dp - delta)).astype(BF16)
            dv_t = jnp.dot(pb, do2, preferred_element_type=F32)
            dk_t = jnp.dot(ds, q2, preferred_element_type=F32)
            dk = dk_t if dk is None else dk + dk_t
            dv = dv_t if dv is None else dv + dv_t
            dq = lax.dot_general(ds, keys, (((0,), (0,)), ((), ())), preferred_element_type=F32)
            dq_ref[:, c0] = dqin_ref[:, c0] + dq[:ROWS] * SCALE
            dq_ref[:, c1] = dqin_ref[:, c1] + dq[ROWS:] * SCALE
        dk = (dk * SCALE).astype(BF16)
        dv = dv.astype(BF16)
        terms_ref[0, :, at] = dk[:ROWS]
        terms_ref[1, :, at] = dk[ROWS:]
        terms_ref[0, :, at_v] = dv[:ROWS]
        terms_ref[1, :, at_v] = dv[ROWS:]


def attend(shift, spans, q, do, lse2, delta, kvp, dq_in, alias):
    vmem = pl.BlockSpec(memory_space=pltpu.VMEM)
    return pl.pallas_call(
        lambda *refs: attend_body(shift, *refs),
        in_specs=[pl.BlockSpec(memory_space=pltpu.SMEM)] + [vmem] * 6,
        out_specs=[vmem] * 2,
        out_shape=[
            jax.ShapeDtypeStruct((2, ROWS, 512), BF16),
            jax.ShapeDtypeStruct((ROWS, 2048), F32),
        ],
        input_output_aliases={6: 1} if alias else {},
        compiler_params=pltpu.CompilerParams(vmem_limit_bytes=24 * MIB),
        cost_estimate=SMALL,
        name="attend",
    )(spans, q, do, lse2, delta, kvp, dq_in)


def dx_body(own_ref, other_ref, *refs):
    w_refs, out_refs, (wz, dk) = refs[:8], refs[8:-2], refs[-2:]
    rows = len(out_refs) * ROWS
    yl = lax.axis_index("yl")
    z = lax.axis_index("z")
    core = lax.axis_index("core")
    for k, ref in enumerate(w_refs):
        wz[lax.rem(z + 8 - k, 8)] = ref[...]
    dk[core] = own_ref[...].reshape(rows, 512)
    dk[1 - core] = other_ref[...].reshape(rows, 512)
    nt = (((1,), (1,)), ((), ()))
    for tile in range(4):
        beta = lax.bitwise_xor(yl, tile // 2)
        total = None
        for half in range(2):
            piece = beta * 2 + lax.bitwise_xor(core, half)
            w = jnp.concatenate([wz[(tile % 2) * 4 + m, piece] for m in range(4)], axis=0)
            got = lax.dot_general(dk[half], w, nt, preferred_element_type=F32)
            total = got if total is None else total + got
        total = total.astype(BF16)
        for n, ref in enumerate(out_refs):
            ref[:, tile * 256 : (tile + 1) * 256] = total[n * ROWS : (n + 1) * ROWS]


def dx_parts(own, other, weights):
    count = own.shape[0]
    vmem = pl.BlockSpec(memory_space=pltpu.VMEM)
    return pl.pallas_call(
        dx_body,
        in_specs=[vmem] * 10,
        out_specs=[vmem] * count,
        out_shape=[jax.ShapeDtypeStruct((ROWS, 1024), BF16)] * count,
        scratch_shapes=[pltpu.VMEM((8, 4, 64, 512), BF16), pltpu.VMEM((2, count * ROWS, 512), BF16)],
        compiler_params=pltpu.CompilerParams(vmem_limit_bytes=24 * MIB),
        cost_estimate=SMALL,
        name="input_grad",
    )(own, other, *weights)


def gather_body(*refs):
    out_ref = refs[4]
    x = lax.axis_index("x")
    for s in range(4):
        to = lax.rem(x + s, 4) * 1024
        out_ref[:, pl.ds(pl.multiple_of(to, 1024), 1024)] = refs[s][...]


def shards(queries, out_grad, outputs, log_norm, kv_held, span_order, dq_acc, dkv_acc, kv_weight):
    vmem = pl.BlockSpec(memory_space=pltpu.VMEM)
    both = permute(jnp.concatenate([kv_held, kv_weight], axis=0), lambda a, x, b, z, h: (1 - a, x, b, z, h))
    core = lax.axis_index("core")

    def step(value, by):
        return permute(value, lambda a, x, b, z, h: (a, x, b, (z + by) % 8, h))

    delta, lse2 = pl.pallas_call(
        delta_body,
        in_specs=[vmem] * 3,
        out_specs=[vmem] * 2,
        out_shape=[jax.ShapeDtypeStruct((16, ROWS), F32)] * 2,
        cost_estimate=SMALL,
        name="row_sums",
    )(out_grad, outputs, log_norm)
    both, delta, lse2 = lax.optimization_barrier((both, delta, lse2))
    pair = jnp.stack([kv_held, both[:ROWS]]).reshape(2, ROWS, 512)
    pairs = {s: permute(pair, along_x(s)) for s in (1, 3, 2)}

    mine = kv_weight.reshape(1, 64, 512)
    theirs = both[ROWS:].reshape(1, 64, 512)
    same = core == lax.axis_index("yh")
    kept, sent = jnp.where(same, mine, theirs), jnp.where(same, theirs, mine)
    w = jnp.concatenate([kept, permute(sent, lambda a, x, b, z, h: (a, x, b, z, 1 - h))], axis=0)
    w = jnp.concatenate([w, permute(w, lambda a, x, b, z, h: (a, x, 1 - b, z, h))], axis=0)
    f1, g1 = step(w, 1), step(w, -1)
    t0, dq = attend(0, span_order, queries, out_grad, lse2, delta, pair, dq_acc, False)
    t1, dq = attend(1, span_order, queries, out_grad, lse2, delta, pairs[1], dq, True)
    back1 = permute(t1, along_x(-1))
    dq, f1, g1 = lax.optimization_barrier((dq, f1, g1))
    f2, g2 = step(f1, 1), step(g1, -1)
    t3, dq = attend(3, span_order, queries, out_grad, lse2, delta, pairs[3], dq, True)
    back3 = permute(t3, along_x(-3))
    dq, back1, f2, g2 = lax.optimization_barrier((dq, back1, f2, g2))
    f3, g3 = step(f2, 1), step(g2, -1)
    t2, dq = attend(2, span_order, queries, out_grad, lse2, delta, pairs[2], dq, True)
    back2 = permute(t2, along_x(-2))
    back2, f3, g3 = lax.optimization_barrier((back2, f3, g3))
    f4 = step(f3, 1)
    back = (t0, back1, back3, back2)
    total = sum(t.astype(F32) for t in back).astype(BF16)
    r0, r1 = total[0], total[1]
    r0 = permute(r0, next_outer(0))
    r1 = permute(r1, next_outer(1))
    r0, f4 = lax.optimization_barrier((r0, f4))
    weights = [w, f1, f2, f3, f4, g3, g2, g1]
    dkv = dkv_acc.reshape(ROWS, 512) + (r0.astype(F32) + r1.astype(F32))
    dkvb = dkv.astype(BF16)

    swap = lambda a, x, b, z, h: (a, x, b, z, 1 - h)
    near = jnp.stack([permute(dkvb, along_x(s)) for s in (1, 2, 3)])
    alone = dkvb[None]
    parts = dx_parts(near, permute(near, swap), weights)
    got = [permute(part, along_x(-s)) for s, part in zip((1, 2, 3), parts)]
    own = dx_parts(alone, permute(alone, swap), weights)
    dx = pl.pallas_call(
        gather_body,
        in_specs=[vmem] * 4,
        out_specs=vmem,
        out_shape=jax.ShapeDtypeStruct((ROWS, 4096), BF16),
        cost_estimate=SMALL,
        name="join_parts",
    )(own[0], *got)
    return (dq, dkv.reshape(ROWS, 2, 256), dx)


def solution(mesh):
    fine = Mesh(mesh.devices.reshape(SIZES), AXES)
    tokens = ("yh", "x", "yl", "z")
    return jax.shard_map(
        shards,
        mesh=fine,
        in_specs=(
            P(tokens, "core"),
            P(tokens, "core"),
            P(tokens, "core"),
            P("core", tokens),
            P(tokens, None, "core"),
            P(),
            P(tokens, "core"),
            P(tokens, None, "core"),
            P(tokens, None, "core"),
        ),
        out_specs=(P(tokens, "core"), P(tokens, None, "core"), P(tokens, "core")),
        check_vma=False,
    )
```

```python
import math

import jax
import jax.numpy as jnp
from jax import lax
from jax.experimental import pallas as pl
from jax.experimental.pallas import tpu as pltpu
from jax.sharding import Mesh, PartitionSpec as P

HD = 128
SPAN = 64
ROWS = 128
AXES = ("yh", "x", "yl", "z", "core")
SIZES = (2, 4, 2, 8, 2)
LOG2E = math.log2(math.e)
SCALE = 1.0 / math.sqrt(HD)
F32 = jnp.float32
BF16 = jnp.bfloat16
MIB = 1 << 20
SMALL = pl.CostEstimate(flops=1000, bytes_accessed=1000, transcendentals=0)


def permute(value, move):
    pairs = []
    for a in range(2):
        for x in range(4):
            for b in range(2):
                for z in range(8):
                    for h in range(2):
                        flat = lambda c: (((c[0] * 4 + c[1]) * 2 + c[2]) * 8 + c[3]) * 2 + c[4]
                        pairs.append((flat((a, x, b, z, h)), flat(move(a, x, b, z, h))))
    return lax.ppermute(value, AXES, pairs)


def along_x(steps):
    return lambda a, x, b, z, h: (a, (x + steps) % 4, b, z, h)


def next_outer(flip):
    def move(a, x, b, z, h):
        g = (b * 8 + z + 1) % 16
        return (a ^ flip, x, g // 8, g % 8, h)

    return move


def delta_body(do_ref, o_ref, lse_ref, delta_ref, lse2_ref):
    ones = jnp.ones((8, HD), F32)
    for h in range(16):
        cols = slice(h * HD, (h + 1) * HD)
        prod = do_ref[:, cols].astype(F32) * o_ref[:, cols].astype(F32)
        row = lax.dot_general(
            ones, prod, (((1,), (1,)), ((), ())),
            precision=lax.Precision.HIGHEST, preferred_element_type=F32,
        )
        delta_ref[h : h + 1, :] = row[0:1]
    lse2_ref[...] = lse_ref[...] * LOG2E


def attend_body(shift, spans, q_ref, do_ref, lse_ref, delta_ref, kv_ref, terms_ref, ds_ref):
    yh = lax.axis_index("yh")
    x = lax.axis_index("x")
    outer = lax.axis_index("yl") * 8 + lax.axis_index("z")
    mine = (yh * 4 + x) * 16 + outer
    key_outer = lax.rem(outer + 1, 16)
    key_x = lax.rem(x + 4 - shift, 4)
    first = (yh * 4 + key_x) * 16 + key_outer
    second = ((1 - yh) * 4 + key_x) * 16 + key_outer
    lane = lax.broadcasted_iota(jnp.int32, (1, ROWS), 1)
    q_pos = jnp.where(lane < SPAN, spans[2 * mine] * SPAN + lane, spans[2 * mine + 1] * SPAN + lane - SPAN)
    row = lax.broadcasted_iota(jnp.int32, (2 * ROWS, 1), 0)
    k_span = jnp.where(
        row < 2 * SPAN,
        jnp.where(row < SPAN, spans[2 * first], spans[2 * first + 1]),
        jnp.where(row < 3 * SPAN, spans[2 * second], spans[2 * second + 1]),
    )
    k_pos = k_span * SPAN + lax.rem(row, SPAN)
    allowed = k_pos <= q_pos
    allowed = jnp.concatenate([allowed, allowed], axis=1)
    nt = (((1,), (1,)), ((), ()))
    for head in range(2):
        at = slice(head * HD, (head + 1) * HD)
        at_v = slice(head * HD + 2 * HD, head * HD + 3 * HD)
        keys = jnp.concatenate([kv_ref[0, :, at], kv_ref[1, :, at]], axis=0)
        values = jnp.concatenate([kv_ref[0, :, at_v], kv_ref[1, :, at_v]], axis=0)
        dk = dv = None
        for pair in range(4):
            h0 = head * 8 + pair * 2
            c0 = slice(h0 * HD, (h0 + 1) * HD)
            c1 = slice((h0 + 1) * HD, (h0 + 2) * HD)
            q2 = jnp.concatenate([q_ref[:, c0], q_ref[:, c1]], axis=0)
            do2 = jnp.concatenate([do_ref[:, c0], do_ref[:, c1]], axis=0)
            lse = jnp.concatenate([lse_ref[h0 : h0 + 1, :], lse_ref[h0 + 1 : h0 + 2, :]], axis=1)
            delta = jnp.concatenate([delta_ref[h0 : h0 + 1, :], delta_ref[h0 + 1 : h0 + 2, :]], axis=1)
            s = lax.dot_general(keys, q2, nt, preferred_element_type=F32)
            dp = lax.dot_general(values, do2, nt, preferred_element_type=F32)
            p = jnp.where(allowed, jnp.exp2(s * (SCALE * LOG2E) - lse), 0.0)
            pb = p.astype(BF16)
            ds = (p * (dp - delta)).astype(BF16)
            dv_t = jnp.dot(pb, do2, preferred_element_type=F32)
            dk_t = jnp.dot(ds, q2, preferred_element_type=F32)
            dk = dk_t if dk is None else dk + dk_t
            dv = dv_t if dv is None else dv + dv_t
            ds_ref[:, h0 * HD : (h0 + 2) * HD] = ds
        dk = (dk * SCALE).astype(BF16)
        dv = dv.astype(BF16)
        terms_ref[0, :, at] = dk[:ROWS]
        terms_ref[1, :, at] = dk[ROWS:]
        terms_ref[0, :, at_v] = dv[:ROWS]
        terms_ref[1, :, at_v] = dv[ROWS:]


def attend(shift, spans, q, do, lse2, delta, kvp):
    vmem = pl.BlockSpec(memory_space=pltpu.VMEM)
    return pl.pallas_call(
        lambda *refs: attend_body(shift, *refs),
        in_specs=[pl.BlockSpec(memory_space=pltpu.SMEM)] + [vmem] * 5,
        out_specs=[vmem] * 2,
        out_shape=[
            jax.ShapeDtypeStruct((2, ROWS, 512), BF16),
            jax.ShapeDtypeStruct((2 * ROWS, 2048), BF16),
        ],
        compiler_params=pltpu.CompilerParams(vmem_limit_bytes=24 * MIB),
        cost_estimate=SMALL,
        name="attend",
    )(spans, q, do, lse2, delta, kvp)


def dq_body(*refs):
    kv_refs, ds_refs, acc_ref, out_ref = refs[:4], refs[4:8], refs[8], refs[9]
    for head in range(2):
        at = slice(head * HD, (head + 1) * HD)
        keys = [jnp.concatenate([kv[0, :, at], kv[1, :, at]], axis=0).T for kv in kv_refs]
        for pair in range(4):
            h0 = head * 8 + pair * 2
            total = None
            for k in range(4):
                got = jnp.dot(keys[k], ds_refs[k][:, h0 * HD : (h0 + 2) * HD], preferred_element_type=F32)
                total = got if total is None else total + got
            for n in range(2):
                cols = slice((h0 + n) * HD, (h0 + n + 1) * HD)
                out_ref[:, cols] = acc_ref[:, cols] + total[:, n * HD : (n + 1) * HD].T * SCALE


def dx_body(own_ref, other_ref, *refs):
    w_refs, out_refs, (wz, dk) = refs[:8], refs[8:-2], refs[-2:]
    rows = len(out_refs) * ROWS
    yl = lax.axis_index("yl")
    z = lax.axis_index("z")
    core = lax.axis_index("core")
    for k, ref in enumerate(w_refs):
        wz[lax.rem(z + 8 - k, 8)] = ref[...]
    dk[core] = own_ref[...].reshape(rows, 512)
    dk[1 - core] = other_ref[...].reshape(rows, 512)
    nt = (((1,), (1,)), ((), ()))
    for tile in range(4):
        beta = lax.bitwise_xor(yl, tile // 2)
        total = None
        for half in range(2):
            piece = beta * 2 + lax.bitwise_xor(core, half)
            w = jnp.concatenate([wz[(tile % 2) * 4 + m, piece] for m in range(4)], axis=0)
            got = lax.dot_general(dk[half], w, nt, preferred_element_type=F32)
            total = got if total is None else total + got
        total = total.astype(BF16)
        for n, ref in enumerate(out_refs):
            ref[:, tile * 256 : (tile + 1) * 256] = total[n * ROWS : (n + 1) * ROWS]


def dx_parts(own, other, weights):
    count = own.shape[0]
    vmem = pl.BlockSpec(memory_space=pltpu.VMEM)
    return pl.pallas_call(
        dx_body,
        in_specs=[vmem] * 10,
        out_specs=[vmem] * count,
        out_shape=[jax.ShapeDtypeStruct((ROWS, 1024), BF16)] * count,
        scratch_shapes=[pltpu.VMEM((8, 4, 64, 512), BF16), pltpu.VMEM((2, count * ROWS, 512), BF16)],
        compiler_params=pltpu.CompilerParams(vmem_limit_bytes=24 * MIB),
        cost_estimate=SMALL,
        name="input_grad",
    )(own, other, *weights)


def gather_body(p0, p1, p2, p3, out_ref, sems):
    x = lax.axis_index("x")
    copies = []
    for s, ref in enumerate((p0, p1, p2, p3)):
        to = pl.multiple_of(lax.rem(x + s, 4) * 1024, 1024)
        copies.append(pltpu.make_async_copy(ref, out_ref.at[:, pl.ds(to, 1024)], sems.at[s]))
    for copy in copies:
        copy.start()
    for copy in copies:
        copy.wait()


def shards(queries, out_grad, outputs, log_norm, kv_held, span_order, dq_acc, dkv_acc, kv_weight):
    vmem = pl.BlockSpec(memory_space=pltpu.VMEM)
    across = lambda a, x, b, z, h: (1 - a, x, b, z, h)
    kvy = permute(kv_held, across)
    mine = kv_weight.reshape(1, 64, 512)
    theirs = permute(mine, across)
    core = lax.axis_index("core")

    def step(value, by):
        return permute(value, lambda a, x, b, z, h: (a, x, b, (z + by) % 8, h))

    delta, lse2 = pl.pallas_call(
        delta_body,
        in_specs=[vmem] * 3,
        out_specs=[vmem] * 2,
        out_shape=[jax.ShapeDtypeStruct((16, ROWS), F32)] * 2,
        cost_estimate=SMALL,
        name="row_sums",
    )(out_grad, outputs, log_norm)
    kvy, delta, lse2 = lax.optimization_barrier((kvy, delta, lse2))
    pair = jnp.stack([kv_held, kvy]).reshape(2, ROWS, 512)
    pairs = {s: permute(pair, along_x(s)) for s in (1, 3, 2)}

    def run(s, kvp):
        return attend(s, span_order, queries, out_grad, lse2, delta, kvp)

    pair, theirs = lax.optimization_barrier((pair, theirs))
    same = core == lax.axis_index("yh")
    kept, sent = jnp.where(same, mine, theirs), jnp.where(same, theirs, mine)
    w = jnp.concatenate([kept, permute(sent, lambda a, x, b, z, h: (a, x, b, z, 1 - h))], axis=0)
    w = jnp.concatenate([w, permute(w, lambda a, x, b, z, h: (a, x, 1 - b, z, h))], axis=0)
    f1, g1 = step(w, 1), step(w, -1)
    pairs[1], pairs[3], pairs[2] = lax.optimization_barrier((pairs[1], pairs[3], pairs[2]))
    t1, ds1 = run(1, pairs[1])
    back1 = permute(t1, along_x(-1))
    ds1, pairs[3] = lax.optimization_barrier((ds1, pairs[3]))
    t3, ds3 = run(3, pairs[3])
    back3 = permute(t3, along_x(-3))
    ds3, pairs[2], f1, g1 = lax.optimization_barrier((ds3, pairs[2], f1, g1))
    t2, ds2 = run(2, pairs[2])
    back2 = permute(t2, along_x(-2))
    f2, g2 = step(f1, 1), step(g1, -1)
    ds2, own_pair = lax.optimization_barrier((ds2, pair))
    t0, ds0 = run(0, own_pair)
    back2, f2, g2 = lax.optimization_barrier((back2, f2, g2))
    f3, g3 = step(f2, 1), step(g2, -1)
    back = (t0, back1, back3, back2)
    dq = pl.pallas_call(
        dq_body,
        in_specs=[vmem] * 9,
        out_specs=vmem,
        out_shape=jax.ShapeDtypeStruct((ROWS, 2048), F32),
        compiler_params=pltpu.CompilerParams(vmem_limit_bytes=24 * MIB),
        cost_estimate=pl.CostEstimate(flops=1000, bytes_accessed=12_000_000, transcendentals=0),
        name="query_grad",
    )(pair, pairs[1], pairs[3], pairs[2], ds0, ds1, ds3, ds2, dq_acc)
    total = sum(t.astype(F32) for t in back).astype(BF16)
    r0, r1 = total[0], total[1]
    r0 = permute(r0, next_outer(0))
    r1 = permute(r1, next_outer(1))
    r0, f3, g3, dq = lax.optimization_barrier((r0, f3, g3, dq))
    f4 = step(f3, 1)
    dkv = dkv_acc.reshape(ROWS, 512) + (r0.astype(F32) + r1.astype(F32))
    dkvb = dkv.astype(BF16)

    swap = lambda a, x, b, z, h: (a, x, b, z, 1 - h)
    near = jnp.stack([permute(dkvb, along_x(s)) for s in (1, 2, 3)])
    near, f4 = lax.optimization_barrier((near, f4))
    weights = [w, f1, f2, f3, f4, g3, g2, g1]
    alone = dkvb[None]
    parts = dx_parts(near, permute(near, swap), weights)
    got = [permute(part, along_x(-s)) for s, part in zip((1, 2, 3), parts)]
    own = dx_parts(alone, permute(alone, swap), weights)
    dx = pl.pallas_call(
        gather_body,
        in_specs=[vmem] * 4,
        out_specs=pl.BlockSpec(memory_space=pl.ANY),
        out_shape=jax.ShapeDtypeStruct((ROWS, 4096), BF16),
        scratch_shapes=[pltpu.SemaphoreType.DMA((4,))],
        cost_estimate=SMALL,
        name="join_parts",
    )(own[0], *got)
    return (dq, dkv.reshape(ROWS, 2, 256), dx)


def solution(mesh):
    fine = Mesh(mesh.devices.reshape(SIZES), AXES)
    tokens = ("yh", "x", "yl", "z")
    return jax.shard_map(
        shards,
        mesh=fine,
        in_specs=(
            P(tokens, "core"),
            P(tokens, "core"),
            P(tokens, "core"),
            P("core", tokens),
            P(tokens, None, "core"),
            P(),
            P(tokens, "core"),
            P(tokens, None, "core"),
            P(tokens, None, "core"),
        ),
        out_specs=(P(tokens, "core"), P(tokens, None, "core"), P(tokens, "core")),
        check_vma=False,
    )
```

```python
import math

import jax
import jax.numpy as jnp
from jax import lax
from jax.experimental import pallas as pl
from jax.experimental.pallas import tpu as pltpu
from jax.sharding import Mesh, PartitionSpec as P

HD = 128
SPAN = 64
ROWS = 128
AXES = ("yh", "x", "yl", "z", "core")
SIZES = (2, 4, 2, 8, 2)
LOG2E = math.log2(math.e)
SCALE = 1.0 / math.sqrt(HD)
F32 = jnp.float32
BF16 = jnp.bfloat16
MIB = 1 << 20
SMALL = pl.CostEstimate(flops=1000, bytes_accessed=1000, transcendentals=0)


def permute(value, move):
    pairs = []
    for a in range(2):
        for x in range(4):
            for b in range(2):
                for z in range(8):
                    for h in range(2):
                        flat = lambda c: (((c[0] * 4 + c[1]) * 2 + c[2]) * 8 + c[3]) * 2 + c[4]
                        pairs.append((flat((a, x, b, z, h)), flat(move(a, x, b, z, h))))
    return lax.ppermute(value, AXES, pairs)


def along_x(steps):
    return lambda a, x, b, z, h: (a, (x + steps) % 4, b, z, h)


def next_outer(flip):
    def move(a, x, b, z, h):
        g = (b * 8 + z + 1) % 16
        return (a ^ flip, x, g // 8, g % 8, h)

    return move


def delta_body(do_ref, o_ref, lse_ref, delta_ref, lse2_ref):
    ones = jnp.ones((8, HD), F32)
    for h in range(16):
        cols = slice(h * HD, (h + 1) * HD)
        prod = do_ref[:, cols].astype(F32) * o_ref[:, cols].astype(F32)
        row = lax.dot_general(
            ones, prod, (((1,), (1,)), ((), ())),
            precision=lax.Precision.HIGHEST, preferred_element_type=F32,
        )
        delta_ref[h : h + 1, :] = row[0:1]
    lse2_ref[...] = lse_ref[...] * LOG2E


def attend_body(shift, spans, q_ref, do_ref, lse_ref, delta_ref, kv_ref, terms_ref, ds_ref):
    yh = lax.axis_index("yh")
    x = lax.axis_index("x")
    outer = lax.axis_index("yl") * 8 + lax.axis_index("z")
    mine = (yh * 4 + x) * 16 + outer
    key_outer = lax.rem(outer + 1, 16)
    key_x = lax.rem(x + 4 - shift, 4)
    first = (yh * 4 + key_x) * 16 + key_outer
    second = ((1 - yh) * 4 + key_x) * 16 + key_outer
    lane = lax.broadcasted_iota(jnp.int32, (1, ROWS), 1)
    q_pos = jnp.where(lane < SPAN, spans[2 * mine] * SPAN + lane, spans[2 * mine + 1] * SPAN + lane - SPAN)
    row = lax.broadcasted_iota(jnp.int32, (2 * ROWS, 1), 0)
    k_span = jnp.where(
        row < 2 * SPAN,
        jnp.where(row < SPAN, spans[2 * first], spans[2 * first + 1]),
        jnp.where(row < 3 * SPAN, spans[2 * second], spans[2 * second + 1]),
    )
    k_pos = k_span * SPAN + lax.rem(row, SPAN)
    allowed = k_pos <= q_pos
    allowed = jnp.concatenate([allowed, allowed], axis=1)
    nt = (((1,), (1,)), ((), ()))
    for head in range(2):
        at = slice(head * HD, (head + 1) * HD)
        at_v = slice(head * HD + 2 * HD, head * HD + 3 * HD)
        keys = jnp.concatenate([kv_ref[0, :, at], kv_ref[1, :, at]], axis=0)
        values = jnp.concatenate([kv_ref[0, :, at_v], kv_ref[1, :, at_v]], axis=0)
        dk = dv = None
        for pair in range(4):
            h0 = head * 8 + pair * 2
            c0 = slice(h0 * HD, (h0 + 1) * HD)
            c1 = slice((h0 + 1) * HD, (h0 + 2) * HD)
            q2 = jnp.concatenate([q_ref[:, c0], q_ref[:, c1]], axis=0)
            do2 = jnp.concatenate([do_ref[:, c0], do_ref[:, c1]], axis=0)
            lse = jnp.concatenate([lse_ref[h0 : h0 + 1, :], lse_ref[h0 + 1 : h0 + 2, :]], axis=1)
            delta = jnp.concatenate([delta_ref[h0 : h0 + 1, :], delta_ref[h0 + 1 : h0 + 2, :]], axis=1)
            s = lax.dot_general(keys, q2, nt, preferred_element_type=F32)
            dp = lax.dot_general(values, do2, nt, preferred_element_type=F32)
            p = jnp.where(allowed, jnp.exp2(s * (SCALE * LOG2E) - lse), 0.0)
            pb = p.astype(BF16)
            ds = (p * (dp - delta)).astype(BF16)
            dv_t = jnp.dot(pb, do2, preferred_element_type=F32)
            dk_t = jnp.dot(ds, q2, preferred_element_type=F32)
            dk = dk_t if dk is None else dk + dk_t
            dv = dv_t if dv is None else dv + dv_t
            ds_ref[:, h0 * HD : (h0 + 2) * HD] = ds
        dk = (dk * SCALE).astype(BF16)
        dv = dv.astype(BF16)
        terms_ref[0, :, at] = dk[:ROWS]
        terms_ref[1, :, at] = dk[ROWS:]
        terms_ref[0, :, at_v] = dv[:ROWS]
        terms_ref[1, :, at_v] = dv[ROWS:]


def attend(shift, spans, q, do, lse2, delta, kvp):
    vmem = pl.BlockSpec(memory_space=pltpu.VMEM)
    return pl.pallas_call(
        lambda *refs: attend_body(shift, *refs),
        in_specs=[pl.BlockSpec(memory_space=pltpu.SMEM)] + [vmem] * 5,
        out_specs=[vmem] * 2,
        out_shape=[
            jax.ShapeDtypeStruct((2, ROWS, 512), BF16),
            jax.ShapeDtypeStruct((2 * ROWS, 2048), BF16),
        ],
        compiler_params=pltpu.CompilerParams(vmem_limit_bytes=24 * MIB),
        cost_estimate=SMALL,
        name="attend",
    )(spans, q, do, lse2, delta, kvp)


def dq_body(*refs):
    kv_refs, ds_refs, acc_ref, out_ref = refs[:4], refs[4:8], refs[8], refs[9]
    for head in range(2):
        at = slice(head * HD, (head + 1) * HD)
        keys = [jnp.concatenate([kv[0, :, at], kv[1, :, at]], axis=0).T for kv in kv_refs]
        for pair in range(4):
            h0 = head * 8 + pair * 2
            total = None
            for k in range(4):
                got = jnp.dot(keys[k], ds_refs[k][:, h0 * HD : (h0 + 2) * HD], preferred_element_type=F32)
                total = got if total is None else total + got
            for n in range(2):
                cols = slice((h0 + n) * HD, (h0 + n + 1) * HD)
                out_ref[:, cols] = acc_ref[:, cols] + total[:, n * HD : (n + 1) * HD].T * SCALE


def dx_body(own_ref, other_ref, *refs):
    w_refs, out_refs, (wz, dk) = refs[:9], refs[9:-2], refs[-2:]
    rows = len(out_refs) * ROWS
    yl = lax.axis_index("yl")
    z = lax.axis_index("z")
    core = lax.axis_index("core")
    for k, ref in zip((0, 1, 2, 3, 5, 6, 7), w_refs[:4] + w_refs[6:]):
        wz[lax.rem(z + 8 - k, 8)] = ref[...]
    far = lax.rem(z + 4, 8)
    wz[far, 0:2] = w_refs[4][...]
    wz[far, 2:4] = w_refs[5][...]
    dk[core] = own_ref[...].reshape(rows, 512)
    dk[1 - core] = other_ref[...].reshape(rows, 512)
    nt = (((1,), (1,)), ((), ()))
    for tile in range(4):
        beta = lax.bitwise_xor(yl, tile // 2)
        total = None
        for half in range(2):
            piece = beta * 2 + lax.bitwise_xor(core, half)
            w = jnp.concatenate([wz[(tile % 2) * 4 + m, piece] for m in range(4)], axis=0)
            got = lax.dot_general(dk[half], w, nt, preferred_element_type=F32)
            total = got if total is None else total + got
        total = total.astype(BF16)
        for n, ref in enumerate(out_refs):
            ref[:, tile * 256 : (tile + 1) * 256] = total[n * ROWS : (n + 1) * ROWS]


def dx_parts(own, other, weights):
    count = own.shape[0]
    vmem = pl.BlockSpec(memory_space=pltpu.VMEM)
    return pl.pallas_call(
        dx_body,
        in_specs=[vmem] * 11,
        out_specs=[vmem] * count,
        out_shape=[jax.ShapeDtypeStruct((ROWS, 1024), BF16)] * count,
        scratch_shapes=[pltpu.VMEM((8, 4, 64, 512), BF16), pltpu.VMEM((2, count * ROWS, 512), BF16)],
        compiler_params=pltpu.CompilerParams(vmem_limit_bytes=24 * MIB),
        cost_estimate=SMALL,
        name="input_grad",
    )(own, other, *weights)


def gather_body(p0, p1, p2, p3, out_ref, sems):
    x = lax.axis_index("x")
    copies = []
    for s, ref in enumerate((p0, p1, p2, p3)):
        to = pl.multiple_of(lax.rem(x + s, 4) * 1024, 1024)
        copies.append(pltpu.make_async_copy(ref, out_ref.at[:, pl.ds(to, 1024)], sems.at[s]))
    for copy in copies:
        copy.start()
    for copy in copies:
        copy.wait()


def shards(queries, out_grad, outputs, log_norm, kv_held, span_order, dq_acc, dkv_acc, kv_weight):
    vmem = pl.BlockSpec(memory_space=pltpu.VMEM)
    across = lambda a, x, b, z, h: (1 - a, x, b, z, h)
    kvy = permute(kv_held, across)
    mine = kv_weight.reshape(1, 64, 512)
    theirs = permute(mine, across)
    core = lax.axis_index("core")

    def step(value, by):
        return permute(value, lambda a, x, b, z, h: (a, x, b, (z + by) % 8, h))

    delta, lse2 = pl.pallas_call(
        delta_body,
        in_specs=[vmem] * 3,
        out_specs=[vmem] * 2,
        out_shape=[jax.ShapeDtypeStruct((16, ROWS), F32)] * 2,
        cost_estimate=SMALL,
        name="row_sums",
    )(out_grad, outputs, log_norm)
    kvy, delta, lse2 = lax.optimization_barrier((kvy, delta, lse2))
    pair = jnp.stack([kv_held, kvy]).reshape(2, ROWS, 512)
    pairs = {s: permute(pair, along_x(s)) for s in (1, 3, 2)}

    def run(s, kvp):
        return attend(s, span_order, queries, out_grad, lse2, delta, kvp)

    pair, theirs = lax.optimization_barrier((pair, theirs))
    same = core == lax.axis_index("yh")
    kept, sent = jnp.where(same, mine, theirs), jnp.where(same, theirs, mine)
    w = jnp.concatenate([kept, permute(sent, lambda a, x, b, z, h: (a, x, b, z, 1 - h))], axis=0)
    w = jnp.concatenate([w, permute(w, lambda a, x, b, z, h: (a, x, 1 - b, z, h))], axis=0)
    f1, g1 = step(w, 1), step(w, -1)
    pairs[1], pairs[3] = lax.optimization_barrier((pairs[1], pairs[3]))
    t1, ds1 = run(1, pairs[1])
    back1 = permute(t1, along_x(-1))
    ds1, pairs[3] = lax.optimization_barrier((ds1, pairs[3]))
    t3, ds3 = run(3, pairs[3])
    back3 = permute(t3, along_x(-3))
    ds3, pairs[2] = lax.optimization_barrier((ds3, pairs[2]))
    t2, ds2 = run(2, pairs[2])
    back2 = permute(t2, along_x(-2))
    ds2, own_pair, f1, g1 = lax.optimization_barrier((ds2, pair, f1, g1))
    f2, g2 = step(f1, 1), step(g1, -1)
    t0, ds0 = run(0, own_pair)
    ds0, f2, g2 = lax.optimization_barrier((ds0, f2, g2))
    f3, g3 = step(f2, 1), step(g2, -1)
    back = (t0, back1, back3, back2)
    dq = pl.pallas_call(
        dq_body,
        in_specs=[vmem] * 9,
        out_specs=vmem,
        out_shape=jax.ShapeDtypeStruct((ROWS, 2048), F32),
        compiler_params=pltpu.CompilerParams(vmem_limit_bytes=24 * MIB),
        cost_estimate=pl.CostEstimate(flops=1000, bytes_accessed=12_000_000, transcendentals=0),
        name="query_grad",
    )(pair, pairs[1], pairs[3], pairs[2], ds0, ds1, ds3, ds2, dq_acc)
    total = sum(t.astype(F32) for t in back).astype(BF16)
    r0, r1 = total[0], total[1]
    r0 = permute(r0, next_outer(0))
    r1 = permute(r1, next_outer(1))
    r0, dq = lax.optimization_barrier((r0, dq))
    dkv = dkv_acc.reshape(ROWS, 512) + (r0.astype(F32) + r1.astype(F32))
    dkvb = dkv.astype(BF16)

    swap = lambda a, x, b, z, h: (a, x, b, z, 1 - h)
    dkvb, f3, g3 = lax.optimization_barrier((dkvb, f3, g3))
    f4, g4 = step(f3[:2], 1), step(g3[2:], -1)
    near = jnp.stack([permute(dkvb, along_x(s)) for s in (1, 2, 3)])
    near, f4, g4 = lax.optimization_barrier((near, f4, g4))
    weights = [w, f1, f2, f3, f4, g4, g3, g2, g1]
    alone = dkvb[None]
    parts = dx_parts(near, permute(near, swap), weights)
    got = [permute(part, along_x(-s)) for s, part in zip((1, 2, 3), parts)]
    own = dx_parts(alone, permute(alone, swap), weights)
    dx = pl.pallas_call(
        gather_body,
        in_specs=[vmem] * 4,
        out_specs=pl.BlockSpec(memory_space=pl.ANY),
        out_shape=jax.ShapeDtypeStruct((ROWS, 4096), BF16),
        scratch_shapes=[pltpu.SemaphoreType.DMA((4,))],
        cost_estimate=SMALL,
        name="join_parts",
    )(own[0], *got)
    return (dq, dkv.reshape(ROWS, 2, 256), dx)


def solution(mesh):
    fine = Mesh(mesh.devices.reshape(SIZES), AXES)
    tokens = ("yh", "x", "yl", "z")
    return jax.shard_map(
        shards,
        mesh=fine,
        in_specs=(
            P(tokens, "core"),
            P(tokens, "core"),
            P(tokens, "core"),
            P("core", tokens),
            P(tokens, None, "core"),
            P(),
            P(tokens, "core"),
            P(tokens, None, "core"),
            P(tokens, None, "core"),
        ),
        out_specs=(P(tokens, "core"), P(tokens, None, "core"), P(tokens, "core")),
        check_vma=False,
    )
```

```python
import math

import jax
import jax.numpy as jnp
from jax import lax
from jax.experimental import pallas as pl
from jax.experimental.pallas import tpu as pltpu
from jax.sharding import Mesh, PartitionSpec as P

HD = 128
SPAN = 64
ROWS = 128
AXES = ("yh", "x", "yl", "z", "core")
SIZES = (2, 4, 2, 8, 2)
LOG2E = math.log2(math.e)
SCALE = 1.0 / math.sqrt(HD)
F32 = jnp.float32
BF16 = jnp.bfloat16
MIB = 1 << 20
SMALL = pl.CostEstimate(flops=1000, bytes_accessed=1000, transcendentals=0)


def permute(value, move):
    pairs = []
    for a in range(2):
        for x in range(4):
            for b in range(2):
                for z in range(8):
                    for h in range(2):
                        flat = lambda c: (((c[0] * 4 + c[1]) * 2 + c[2]) * 8 + c[3]) * 2 + c[4]
                        pairs.append((flat((a, x, b, z, h)), flat(move(a, x, b, z, h))))
    return lax.ppermute(value, AXES, pairs)


def along_x(steps):
    return lambda a, x, b, z, h: (a, (x + steps) % 4, b, z, h)


def next_outer(flip):
    def move(a, x, b, z, h):
        g = (b * 8 + z + 1) % 16
        return (a ^ flip, x, g // 8, g % 8, h)

    return move


def delta_body(do_ref, o_ref, lse_ref, delta_ref, lse2_ref):
    ones = jnp.ones((8, 3 * HD), BF16)
    for h in range(16):
        cols = slice(h * HD, (h + 1) * HD)
        rest = do_ref[:, cols].astype(F32) * o_ref[:, cols].astype(F32)
        pieces = []
        for _ in range(3):
            pieces.append(rest.astype(BF16))
            rest = rest - pieces[-1].astype(F32)
        row = lax.dot_general(
            ones, jnp.concatenate(pieces, axis=1), (((1,), (1,)), ((), ())), preferred_element_type=F32
        )
        delta_ref[h : h + 1, :] = row[0:1]
    lse2_ref[...] = lse_ref[...] * LOG2E


def attend_body(shift, spans, q_ref, do_ref, lse_ref, delta_ref, kv_ref, terms_ref, ds_ref):
    yh = lax.axis_index("yh")
    x = lax.axis_index("x")
    outer = lax.axis_index("yl") * 8 + lax.axis_index("z")
    mine = (yh * 4 + x) * 16 + outer
    key_outer = lax.rem(outer + 1, 16)
    key_x = lax.rem(x + 4 - shift, 4)
    first = (yh * 4 + key_x) * 16 + key_outer
    second = ((1 - yh) * 4 + key_x) * 16 + key_outer
    lane = lax.broadcasted_iota(jnp.int32, (1, ROWS), 1)
    q_pos = jnp.where(lane < SPAN, spans[2 * mine] * SPAN + lane, spans[2 * mine + 1] * SPAN + lane - SPAN)
    row = lax.broadcasted_iota(jnp.int32, (2 * ROWS, 1), 0)
    k_span = jnp.where(
        row < 2 * SPAN,
        jnp.where(row < SPAN, spans[2 * first], spans[2 * first + 1]),
        jnp.where(row < 3 * SPAN, spans[2 * second], spans[2 * second + 1]),
    )
    k_pos = k_span * SPAN + lax.rem(row, SPAN)
    allowed = k_pos <= q_pos
    allowed = jnp.concatenate([allowed, allowed], axis=1)
    nt = (((1,), (1,)), ((), ()))
    for head in range(2):
        at = slice(head * HD, (head + 1) * HD)
        at_v = slice(head * HD + 2 * HD, head * HD + 3 * HD)
        keys = jnp.concatenate([kv_ref[0, :, at], kv_ref[1, :, at]], axis=0)
        values = jnp.concatenate([kv_ref[0, :, at_v], kv_ref[1, :, at_v]], axis=0)
        dk = dv = None
        for pair in range(4):
            h0 = head * 8 + pair * 2
            c0 = slice(h0 * HD, (h0 + 1) * HD)
            c1 = slice((h0 + 1) * HD, (h0 + 2) * HD)
            q2 = jnp.concatenate([q_ref[:, c0], q_ref[:, c1]], axis=0)
            do2 = jnp.concatenate([do_ref[:, c0], do_ref[:, c1]], axis=0)
            lse = jnp.concatenate([lse_ref[h0 : h0 + 1, :], lse_ref[h0 + 1 : h0 + 2, :]], axis=1)
            delta = jnp.concatenate([delta_ref[h0 : h0 + 1, :], delta_ref[h0 + 1 : h0 + 2, :]], axis=1)
            s = lax.dot_general(keys, q2, nt, preferred_element_type=F32)
            dp = lax.dot_general(values, do2, nt, preferred_element_type=F32)
            p = jnp.where(allowed, jnp.exp2(s * (SCALE * LOG2E) - lse), 0.0)
            pb = p.astype(BF16)
            ds = (p * (dp - delta)).astype(BF16)
            dv_t = jnp.dot(pb, do2, preferred_element_type=F32)
            dk_t = jnp.dot(ds, q2, preferred_element_type=F32)
            dk = dk_t if dk is None else dk + dk_t
            dv = dv_t if dv is None else dv + dv_t
            ds_ref[:, h0 * HD : (h0 + 2) * HD] = ds
        dk = (dk * SCALE).astype(BF16)
        dv = dv.astype(BF16)
        terms_ref[0, :, at] = dk[:ROWS]
        terms_ref[1, :, at] = dk[ROWS:]
        terms_ref[0, :, at_v] = dv[:ROWS]
        terms_ref[1, :, at_v] = dv[ROWS:]


def attend(shift, spans, q, do, lse2, delta, kvp):
    vmem = pl.BlockSpec(memory_space=pltpu.VMEM)
    return pl.pallas_call(
        lambda *refs: attend_body(shift, *refs),
        in_specs=[pl.BlockSpec(memory_space=pltpu.SMEM)] + [vmem] * 5,
        out_specs=[vmem] * 2,
        out_shape=[
            jax.ShapeDtypeStruct((2, ROWS, 512), BF16),
            jax.ShapeDtypeStruct((2 * ROWS, 2048), BF16),
        ],
        compiler_params=pltpu.CompilerParams(vmem_limit_bytes=24 * MIB),
        cost_estimate=SMALL,
        name="attend",
    )(spans, q, do, lse2, delta, kvp)


def dq_body(*refs):
    kv_refs, ds_refs, acc_ref, out_ref = refs[:4], refs[4:8], refs[8], refs[9]
    for head in range(2):
        at = slice(head * HD, (head + 1) * HD)
        keys = [jnp.concatenate([kv[0, :, at], kv[1, :, at]], axis=0).T for kv in kv_refs]
        for pair in range(4):
            h0 = head * 8 + pair * 2
            total = None
            for k in range(4):
                got = jnp.dot(keys[k], ds_refs[k][:, h0 * HD : (h0 + 2) * HD], preferred_element_type=F32)
                total = got if total is None else total + got
            for n in range(2):
                cols = slice((h0 + n) * HD, (h0 + n + 1) * HD)
                out_ref[:, cols] = acc_ref[:, cols] + total[:, n * HD : (n + 1) * HD].T * SCALE


def dx_body(own_ref, other_ref, *refs):
    w_refs, out_refs, (wz, dk) = refs[:8], refs[8:-2], refs[-2:]
    rows = len(out_refs) * ROWS
    yl = lax.axis_index("yl")
    z = lax.axis_index("z")
    core = lax.axis_index("core")
    for k, ref in enumerate(w_refs):
        wz[lax.rem(z + 8 - k, 8)] = ref[...]
    dk[core] = own_ref[...].reshape(rows, 512)
    dk[1 - core] = other_ref[...].reshape(rows, 512)
    nt = (((1,), (1,)), ((), ()))
    for tile in range(4):
        beta = lax.bitwise_xor(yl, tile // 2)
        total = None
        for half in range(2):
            piece = beta * 2 + lax.bitwise_xor(core, half)
            w = jnp.concatenate([wz[(tile % 2) * 4 + m, piece] for m in range(4)], axis=0)
            got = lax.dot_general(dk[half], w, nt, preferred_element_type=F32)
            total = got if total is None else total + got
        total = total.astype(BF16)
        for n, ref in enumerate(out_refs):
            ref[:, tile * 256 : (tile + 1) * 256] = total[n * ROWS : (n + 1) * ROWS]


def dx_parts(own, other, weights):
    count = own.shape[0]
    vmem = pl.BlockSpec(memory_space=pltpu.VMEM)
    return pl.pallas_call(
        dx_body,
        in_specs=[vmem] * 10,
        out_specs=[vmem] * count,
        out_shape=[jax.ShapeDtypeStruct((ROWS, 1024), BF16)] * count,
        scratch_shapes=[pltpu.VMEM((8, 4, 64, 512), BF16), pltpu.VMEM((2, count * ROWS, 512), BF16)],
        compiler_params=pltpu.CompilerParams(vmem_limit_bytes=24 * MIB),
        cost_estimate=SMALL,
        name="input_grad",
    )(own, other, *weights)


def gather_body(p0, p1, p2, p3, out_ref, sems):
    x = lax.axis_index("x")
    copies = []
    for s, ref in enumerate((p0, p1, p2, p3)):
        to = pl.multiple_of(lax.rem(x + s, 4) * 1024, 1024)
        copies.append(pltpu.make_async_copy(ref, out_ref.at[:, pl.ds(to, 1024)], sems.at[s]))
    for copy in copies:
        copy.start()
    for copy in copies:
        copy.wait()


def shards(queries, out_grad, outputs, log_norm, kv_held, span_order, dq_acc, dkv_acc, kv_weight):
    vmem = pl.BlockSpec(memory_space=pltpu.VMEM)
    across = lambda a, x, b, z, h: (1 - a, x, b, z, h)
    kvy = permute(kv_held, across)
    mine = kv_weight.reshape(1, 64, 512)
    theirs = permute(mine, across)
    core = lax.axis_index("core")

    def step(value, by):
        return permute(value, lambda a, x, b, z, h: (a, x, b, (z + by) % 8, h))

    delta, lse2 = pl.pallas_call(
        delta_body,
        in_specs=[vmem] * 3,
        out_specs=[vmem] * 2,
        out_shape=[jax.ShapeDtypeStruct((16, ROWS), F32)] * 2,
        cost_estimate=SMALL,
        name="row_sums",
    )(out_grad, outputs, log_norm)
    kvy, delta, lse2 = lax.optimization_barrier((kvy, delta, lse2))
    pair = jnp.stack([kv_held, kvy]).reshape(2, ROWS, 512)
    pairs = {s: permute(pair, along_x(s)) for s in (1, 3, 2)}

    def run(s, kvp):
        return attend(s, span_order, queries, out_grad, lse2, delta, kvp)

    pair, theirs = lax.optimization_barrier((pair, theirs))
    same = core == lax.axis_index("yh")
    kept, sent = jnp.where(same, mine, theirs), jnp.where(same, theirs, mine)
    w = jnp.concatenate([kept, permute(sent, lambda a, x, b, z, h: (a, x, b, z, 1 - h))], axis=0)
    w = jnp.concatenate([w, permute(w, lambda a, x, b, z, h: (a, x, 1 - b, z, h))], axis=0)
    f1, g1 = step(w, 1), step(w, -1)
    pairs[1], pairs[3], pairs[2] = lax.optimization_barrier((pairs[1], pairs[3], pairs[2]))
    t1, ds1 = run(1, pairs[1])
    back1 = permute(t1, along_x(-1))
    ds1, pairs[3] = lax.optimization_barrier((ds1, pairs[3]))
    t3, ds3 = run(3, pairs[3])
    back3 = permute(t3, along_x(-3))
    ds3, pairs[2], f1, g1 = lax.optimization_barrier((ds3, pairs[2], f1, g1))
    t2, ds2 = run(2, pairs[2])
    back2 = permute(t2, along_x(-2))
    f2, g2 = step(f1, 1), step(g1, -1)
    ds2, own_pair = lax.optimization_barrier((ds2, pair))
    t0, ds0 = run(0, own_pair)
    back2, f2, g2 = lax.optimization_barrier((back2, f2, g2))
    f3, g3 = step(f2, 1), step(g2, -1)
    back = (t0, back1, back3, back2)
    dq = pl.pallas_call(
        dq_body,
        in_specs=[vmem] * 9,
        out_specs=vmem,
        out_shape=jax.ShapeDtypeStruct((ROWS, 2048), F32),
        compiler_params=pltpu.CompilerParams(vmem_limit_bytes=24 * MIB),
        cost_estimate=pl.CostEstimate(flops=1000, bytes_accessed=12_000_000, transcendentals=0),
        name="query_grad",
    )(pair, pairs[1], pairs[3], pairs[2], ds0, ds1, ds3, ds2, dq_acc)
    total = sum(t.astype(F32) for t in back).astype(BF16)
    r0, r1 = total[0], total[1]
    r0 = permute(r0, next_outer(0))
    r1 = permute(r1, next_outer(1))
    r0, f3, g3, dq = lax.optimization_barrier((r0, f3, g3, dq))
    f4 = step(f3, 1)
    dkv = dkv_acc.reshape(ROWS, 512) + (r0.astype(F32) + r1.astype(F32))
    dkvb = dkv.astype(BF16)

    swap = lambda a, x, b, z, h: (a, x, b, z, 1 - h)
    near = jnp.stack([permute(dkvb, along_x(s)) for s in (1, 2, 3)])
    near, f4 = lax.optimization_barrier((near, f4))
    weights = [w, f1, f2, f3, f4, g3, g2, g1]
    alone = dkvb[None]
    parts = dx_parts(near, permute(near, swap), weights)
    got = [permute(part, along_x(-s)) for s, part in zip((1, 2, 3), parts)]
    own = dx_parts(alone, permute(alone, swap), weights)
    dx = pl.pallas_call(
        gather_body,
        in_specs=[vmem] * 4,
        out_specs=pl.BlockSpec(memory_space=pl.ANY),
        out_shape=jax.ShapeDtypeStruct((ROWS, 4096), BF16),
        scratch_shapes=[pltpu.SemaphoreType.DMA((4,))],
        cost_estimate=SMALL,
        name="join_parts",
    )(own[0], *got)
    return (dq, dkv.reshape(ROWS, 2, 256), dx)


def solution(mesh):
    fine = Mesh(mesh.devices.reshape(SIZES), AXES)
    tokens = ("yh", "x", "yl", "z")
    return jax.shard_map(
        shards,
        mesh=fine,
        in_specs=(
            P(tokens, "core"),
            P(tokens, "core"),
            P(tokens, "core"),
            P("core", tokens),
            P(tokens, None, "core"),
            P(),
            P(tokens, "core"),
            P(tokens, None, "core"),
            P(tokens, None, "core"),
        ),
        out_specs=(P(tokens, "core"), P(tokens, None, "core"), P(tokens, "core")),
        check_vma=False,
    )
```

```python
import math

import jax
import jax.numpy as jnp
from jax import lax
from jax.experimental import pallas as pl
from jax.experimental.pallas import tpu as pltpu
from jax.sharding import Mesh, PartitionSpec as P

HD = 128
SPAN = 64
ROWS = 128
AXES = ("yh", "x", "yl", "z", "core")
SIZES = (2, 4, 2, 8, 2)
LOG2E = math.log2(math.e)
SCALE = 1.0 / math.sqrt(HD)
F32 = jnp.float32
BF16 = jnp.bfloat16
MIB = 1 << 20
SMALL = pl.CostEstimate(flops=1000, bytes_accessed=1000, transcendentals=0)


def permute(value, move):
    pairs = []
    for a in range(2):
        for x in range(4):
            for b in range(2):
                for z in range(8):
                    for h in range(2):
                        flat = lambda c: (((c[0] * 4 + c[1]) * 2 + c[2]) * 8 + c[3]) * 2 + c[4]
                        pairs.append((flat((a, x, b, z, h)), flat(move(a, x, b, z, h))))
    return lax.ppermute(value, AXES, pairs)


def along_x(steps):
    return lambda a, x, b, z, h: (a, (x + steps) % 4, b, z, h)


def next_outer(flip):
    def move(a, x, b, z, h):
        g = (b * 8 + z + 1) % 16
        return (a ^ flip, x, g // 8, g % 8, h)

    return move


def delta_body(do_ref, o_ref, lse_ref, delta_ref, lse2_ref):
    ones = jnp.ones((8, 3 * HD), BF16)
    for h in range(16):
        cols = slice(h * HD, (h + 1) * HD)
        rest = do_ref[:, cols].astype(F32) * o_ref[:, cols].astype(F32)
        pieces = []
        for _ in range(3):
            pieces.append(rest.astype(BF16))
            rest = rest - pieces[-1].astype(F32)
        row = lax.dot_general(
            ones, jnp.concatenate(pieces, axis=1), (((1,), (1,)), ((), ())), preferred_element_type=F32
        )
        delta_ref[h : h + 1, :] = row[0:1]
    lse2_ref[...] = lse_ref[...] * LOG2E


def attend_body(shift, spans, q_ref, do_ref, lse_ref, delta_ref, kv_ref, terms_ref, ds_ref):
    yh = lax.axis_index("yh")
    x = lax.axis_index("x")
    outer = lax.axis_index("yl") * 8 + lax.axis_index("z")
    mine = (yh * 4 + x) * 16 + outer
    key_outer = lax.rem(outer + 1, 16)
    key_x = lax.rem(x + 4 - shift, 4)
    first = (yh * 4 + key_x) * 16 + key_outer
    second = ((1 - yh) * 4 + key_x) * 16 + key_outer
    lane = lax.broadcasted_iota(jnp.int32, (1, ROWS), 1)
    q_pos = jnp.where(lane < SPAN, spans[2 * mine] * SPAN + lane, spans[2 * mine + 1] * SPAN + lane - SPAN)
    row = lax.broadcasted_iota(jnp.int32, (2 * ROWS, 1), 0)
    k_span = jnp.where(
        row < 2 * SPAN,
        jnp.where(row < SPAN, spans[2 * first], spans[2 * first + 1]),
        jnp.where(row < 3 * SPAN, spans[2 * second], spans[2 * second + 1]),
    )
    k_pos = k_span * SPAN + lax.rem(row, SPAN)
    allowed = k_pos <= q_pos
    allowed = jnp.concatenate([allowed, allowed], axis=1)
    nt = (((1,), (1,)), ((), ()))
    for head in range(2):
        at = slice(head * HD, (head + 1) * HD)
        at_v = slice(head * HD + 2 * HD, head * HD + 3 * HD)
        keys = jnp.concatenate([kv_ref[0, :, at], kv_ref[1, :, at]], axis=0)
        values = jnp.concatenate([kv_ref[0, :, at_v], kv_ref[1, :, at_v]], axis=0)
        dk = dv = None
        for pair in range(4):
            h0 = head * 8 + pair * 2
            c0 = slice(h0 * HD, (h0 + 1) * HD)
            c1 = slice((h0 + 1) * HD, (h0 + 2) * HD)
            q2 = jnp.concatenate([q_ref[:, c0], q_ref[:, c1]], axis=0)
            do2 = jnp.concatenate([do_ref[:, c0], do_ref[:, c1]], axis=0)
            lse = jnp.concatenate([lse_ref[h0 : h0 + 1, :], lse_ref[h0 + 1 : h0 + 2, :]], axis=1)
            delta = jnp.concatenate([delta_ref[h0 : h0 + 1, :], delta_ref[h0 + 1 : h0 + 2, :]], axis=1)
            s = lax.dot_general(keys, q2, nt, preferred_element_type=F32)
            dp = lax.dot_general(values, do2, nt, preferred_element_type=F32)
            p = jnp.where(allowed, jnp.exp2(s * (SCALE * LOG2E) - lse), 0.0)
            pb = p.astype(BF16)
            ds = (p * (dp - delta)).astype(BF16)
            dv_t = jnp.dot(pb, do2, preferred_element_type=F32)
            dk_t = jnp.dot(ds, q2, preferred_element_type=F32)
            dk = dk_t if dk is None else dk + dk_t
            dv = dv_t if dv is None else dv + dv_t
            ds_ref[:, h0 * HD : (h0 + 2) * HD] = ds
        dk = (dk * SCALE).astype(BF16)
        dv = dv.astype(BF16)
        terms_ref[0, :, at] = dk[:ROWS]
        terms_ref[1, :, at] = dk[ROWS:]
        terms_ref[0, :, at_v] = dv[:ROWS]
        terms_ref[1, :, at_v] = dv[ROWS:]


def attend(shift, spans, q, do, lse2, delta, kvp):
    vmem = pl.BlockSpec(memory_space=pltpu.VMEM)
    return pl.pallas_call(
        lambda *refs: attend_body(shift, *refs),
        in_specs=[pl.BlockSpec(memory_space=pltpu.SMEM)] + [vmem] * 5,
        out_specs=[vmem] * 2,
        out_shape=[
            jax.ShapeDtypeStruct((2, ROWS, 512), BF16),
            jax.ShapeDtypeStruct((2 * ROWS, 2048), BF16),
        ],
        compiler_params=pltpu.CompilerParams(vmem_limit_bytes=24 * MIB),
        cost_estimate=SMALL,
        name="attend",
    )(spans, q, do, lse2, delta, kvp)


def dq_body(*refs):
    kv_refs, ds_refs, acc_ref, out_ref = refs[:4], refs[4:8], refs[8], refs[9]
    for head in range(2):
        at = slice(head * HD, (head + 1) * HD)
        keys = [jnp.concatenate([kv[0, :, at], kv[1, :, at]], axis=0).T for kv in kv_refs]
        for pair in range(4):
            h0 = head * 8 + pair * 2
            total = None
            for k in range(4):
                got = jnp.dot(keys[k], ds_refs[k][:, h0 * HD : (h0 + 2) * HD], preferred_element_type=F32)
                total = got if total is None else total + got
            for n in range(2):
                cols = slice((h0 + n) * HD, (h0 + n + 1) * HD)
                out_ref[:, cols] = acc_ref[:, cols] + total[:, n * HD : (n + 1) * HD].T * SCALE


def dx_body(own_ref, other_ref, *refs):
    w_refs, out_refs, (wz, dk) = refs[:8], refs[8:-2], refs[-2:]
    rows = len(out_refs) * ROWS
    yl = lax.axis_index("yl")
    z = lax.axis_index("z")
    core = lax.axis_index("core")
    for k, ref in enumerate(w_refs):
        wz[lax.rem(z + 8 - k, 8)] = ref[...]
    dk[core] = own_ref[...].reshape(rows, 512)
    dk[1 - core] = other_ref[...].reshape(rows, 512)
    nt = (((1,), (1,)), ((), ()))
    for tile in range(4):
        beta = lax.bitwise_xor(yl, tile // 2)
        total = None
        for half in range(2):
            piece = beta * 2 + lax.bitwise_xor(core, half)
            w = jnp.concatenate([wz[(tile % 2) * 4 + m, piece] for m in range(4)], axis=0)
            got = lax.dot_general(dk[half], w, nt, preferred_element_type=F32)
            total = got if total is None else total + got
        total = total.astype(BF16)
        for n, ref in enumerate(out_refs):
            ref[:, tile * 256 : (tile + 1) * 256] = total[n * ROWS : (n + 1) * ROWS]


def dx_parts(own, other, weights):
    count = own.shape[0]
    vmem = pl.BlockSpec(memory_space=pltpu.VMEM)
    return pl.pallas_call(
        dx_body,
        in_specs=[vmem] * 10,
        out_specs=[vmem] * count,
        out_shape=[jax.ShapeDtypeStruct((ROWS, 1024), BF16)] * count,
        scratch_shapes=[pltpu.VMEM((8, 4, 64, 512), BF16), pltpu.VMEM((2, count * ROWS, 512), BF16)],
        compiler_params=pltpu.CompilerParams(vmem_limit_bytes=24 * MIB),
        cost_estimate=SMALL,
        name="input_grad",
    )(own, other, *weights)


def gather_body(p0, p1, p2, p3, out_ref, sems):
    x = lax.axis_index("x")
    copies = []
    for s, ref in enumerate((p0, p1, p2, p3)):
        to = pl.multiple_of(lax.rem(x + s, 4) * 1024, 1024)
        copies.append(pltpu.make_async_copy(ref, out_ref.at[:, pl.ds(to, 1024)], sems.at[s]))
    for copy in copies:
        copy.start()
    for copy in copies:
        copy.wait()


def shards(queries, out_grad, outputs, log_norm, kv_held, span_order, dq_acc, dkv_acc, kv_weight):
    vmem = pl.BlockSpec(memory_space=pltpu.VMEM)
    across = lambda a, x, b, z, h: (1 - a, x, b, z, h)
    kvy = permute(kv_held, across)
    mine = kv_weight.reshape(1, 64, 512)
    theirs = permute(mine, across)
    core = lax.axis_index("core")

    def step(value, by):
        return permute(value, lambda a, x, b, z, h: (a, x, b, (z + by) % 8, h))

    delta, lse2 = pl.pallas_call(
        delta_body,
        in_specs=[vmem] * 3,
        out_specs=[vmem] * 2,
        out_shape=[jax.ShapeDtypeStruct((16, ROWS), F32)] * 2,
        cost_estimate=SMALL,
        name="row_sums",
    )(out_grad, outputs, log_norm)
    kvy, delta, lse2 = lax.optimization_barrier((kvy, delta, lse2))
    pair = jnp.stack([kv_held, kvy]).reshape(2, ROWS, 512)
    pairs = {s: permute(pair, along_x(s)) for s in (1, 3, 2)}

    def run(s, kvp):
        return attend(s, span_order, queries, out_grad, lse2, delta, kvp)

    pair, theirs = lax.optimization_barrier((pair, theirs))
    same = core == lax.axis_index("yh")
    kept, sent = jnp.where(same, mine, theirs), jnp.where(same, theirs, mine)
    w = jnp.concatenate([kept, permute(sent, lambda a, x, b, z, h: (a, x, b, z, 1 - h))], axis=0)
    w = jnp.concatenate([w, permute(w, lambda a, x, b, z, h: (a, x, 1 - b, z, h))], axis=0)
    f1, g1 = step(w, 1), step(w, -1)
    pairs[1], pairs[3] = lax.optimization_barrier((pairs[1], pairs[3]))
    t1, ds1 = run(1, pairs[1])
    back1 = permute(t1, along_x(-1))
    ds1, pairs[3] = lax.optimization_barrier((ds1, pairs[3]))
    t3, ds3 = run(3, pairs[3])
    back3 = permute(t3, along_x(-3))
    ds3, pairs[2] = lax.optimization_barrier((ds3, pairs[2]))
    t2, ds2 = run(2, pairs[2])
    back2 = permute(t2, along_x(-2))
    ds2, own_pair, f1, g1 = lax.optimization_barrier((ds2, pair, f1, g1))
    f2, g2 = step(f1, 1), step(g1, -1)
    t0, ds0 = run(0, own_pair)
    back2, f2, g2 = lax.optimization_barrier((back2, f2, g2))
    f3, g3 = step(f2, 1), step(g2, -1)
    back = (t0, back1, back3, back2)
    dq = pl.pallas_call(
        dq_body,
        in_specs=[vmem] * 9,
        out_specs=vmem,
        out_shape=jax.ShapeDtypeStruct((ROWS, 2048), F32),
        compiler_params=pltpu.CompilerParams(vmem_limit_bytes=24 * MIB),
        cost_estimate=pl.CostEstimate(flops=1000, bytes_accessed=12_000_000, transcendentals=0),
        name="query_grad",
    )(pair, pairs[1], pairs[3], pairs[2], ds0, ds1, ds3, ds2, dq_acc)
    total = sum(t.astype(F32) for t in back).astype(BF16)
    r0, r1 = total[0], total[1]
    r0 = permute(r0, next_outer(0))
    r1 = permute(r1, next_outer(1))
    r0, f3, g3, dq = lax.optimization_barrier((r0, f3, g3, dq))
    f4 = step(f3, 1)
    dkv = dkv_acc.reshape(ROWS, 512) + (r0.astype(F32) + r1.astype(F32))
    dkvb = dkv.astype(BF16)

    swap = lambda a, x, b, z, h: (a, x, b, z, 1 - h)
    near = jnp.stack([permute(dkvb, along_x(s)) for s in (1, 2, 3)])
    near, f4 = lax.optimization_barrier((near, f4))
    weights = [w, f1, f2, f3, f4, g3, g2, g1]
    alone = dkvb[None]
    parts = dx_parts(near, permute(near, swap), weights)
    got = [permute(part, along_x(-s)) for s, part in zip((1, 2, 3), parts)]
    own = dx_parts(alone, permute(alone, swap), weights)
    dx = pl.pallas_call(
        gather_body,
        in_specs=[vmem] * 4,
        out_specs=pl.BlockSpec(memory_space=pl.ANY),
        out_shape=jax.ShapeDtypeStruct((ROWS, 4096), BF16),
        scratch_shapes=[pltpu.SemaphoreType.DMA((4,))],
        cost_estimate=SMALL,
        name="join_parts",
    )(own[0], *got)
    return (dq, dkv.reshape(ROWS, 2, 256), dx)


def solution(mesh):
    fine = Mesh(mesh.devices.reshape(SIZES), AXES)
    tokens = ("yh", "x", "yl", "z")
    return jax.shard_map(
        shards,
        mesh=fine,
        in_specs=(
            P(tokens, "core"),
            P(tokens, "core"),
            P(tokens, "core"),
            P("core", tokens),
            P(tokens, None, "core"),
            P(),
            P(tokens, "core"),
            P(tokens, None, "core"),
            P(tokens, None, "core"),
        ),
        out_specs=(P(tokens, "core"), P(tokens, None, "core"), P(tokens, "core")),
        check_vma=False,
    )
```
